1024 devices in a mesh: grp: 32 (over z), dev: 32 (over y, x, core).
Axes of the slice: x: 4, y: 4, z: 32, core: 2. Of those that a mesh axis runs over, the one named last changes fastest.
Arguments:
- basis: float32 [64, 131072], P(None, ('grp', 'dev')), may hold values from -6 to 6
- own_tiles: bfloat16 [1024, 32, 128, 128], P(('grp', 'dev')), may hold values from -0.0625 to 0.0625
- own_col: int32 [1024, 32], P(('grp', 'dev')), may hold values from 0 to 63
- help_tiles: bfloat16 [1024, 32, 2, 128, 128], P(('grp', 'dev')), may hold values from -0.0625 to 0.0625
- help_col: int32 [1024, 32, 2], P(('grp', 'dev')), may hold values from 0 to 31
- help_count: int32 [1024, 32], P(('grp', 'dev')), may hold values from 0 to 2, as said below
Outputs:
- filtered: float32 [64, 131072], P(None, ('grp', 'dev'))
- gram: float32 [64, 64], replicated
The draws below stay inside these ranges and needn't reach their ends.
Inputs may be any that keep to these rules, and one draw needn't show every extreme that they name: `help_count`: each helper row has one row block of its group with all 2 slots live.
All inputs are finite; a program needn't handle non-finite values.
Results may differ from the reference program's by a relative error of at most 0.0034.
Values may be sent and summed in bfloat16 or wider, within the bound.
No kernel may reach another device: no remote copies, remote signals or barrier semaphores. Data moves between devices by JAX's collectives and lax.ppermute only.
A program may use at most 32 MiB of HBM per device.

```python
import jax
import jax.numpy as jnp
from jax import lax

K = 64
TILE = 128
OWN_T = 32
HCAP = 2
DEVS = 1024
GROUP = 32
COLS = 64
TOTAL_ROWS = 131072
N_GRP = 32
N_DEV = 32


def draw_help_count(key, part):
    key = jax.random.fold_in(key, 7)
    first_key, second_key = jax.random.split(key)
    counts = jax.random.randint(first_key, (DEVS, GROUP), 0, HCAP + 1)
    hottest = jax.random.randint(second_key, (DEVS, 1), 0, GROUP)
    places = jnp.arange(GROUP, dtype=jnp.int32)[None, :]
    return jnp.where(places == hottest, HCAP, counts).astype(jnp.int32)


def with_ends(values, key, smallest, top_value):
    shape = values.shape
    index_at = [jax.random.randint(jax.random.fold_in(key, axis), (), 0, shape[axis]) for axis in range(len(shape))]
    values = values.at[tuple(index_at)].set(smallest)
    longest = shape.index(max(shape))
    index_at[longest] = (index_at[longest] + 1) % shape[longest]
    return values.at[tuple(index_at)].set(top_value)


def shard_levels(own_key, dims, cuts, least, high):
    loudness = 1.0
    for axis_at, shards_of in cuts:
        draws = jax.random.uniform(jax.random.fold_in(jax.random.fold_in(own_key, 6), axis_at), (shards_of,), jnp.float32, least / len(cuts), high / len(cuts))
        loudness = loudness * jnp.repeat(jnp.exp(draws), dims[axis_at] // shards_of).reshape((-1,) + (1,) * (len(dims) - 1 - axis_at))
    return loudness


def normal_values(stream_key, shape, spread, reach, shards=(), held_as=jnp.bfloat16):
    array = jax.random.normal(stream_key, shape, jnp.float32) * spread
    if len(shards) > 0:
        array = shard_levels(stream_key, shape, shards, -0.22, 0.18) * array
    return jnp.clip(array, min=-reach, max=reach).astype(held_as)


def setup_inputs(seed: int = 0) -> dict:
    splits = jax.random.split(jax.random.key(seed), 7)
    basis = normal_values(splits[0], (K, TOTAL_ROWS), 1.0, 6.0, ((1, 1024),), jnp.float32)
    own_tiles = normal_values(splits[1], (DEVS, OWN_T, TILE, TILE), (TILE * (OWN_T + N_DEV)) ** -0.5, 0.0625, ((0, 1024),))
    own_col = with_ends(jax.random.randint(splits[2], (DEVS, OWN_T), 0, COLS), jax.random.fold_in(splits[2], 1), 0, COLS - 1).astype(jnp.int32)
    help_tiles = normal_values(splits[3], (DEVS, GROUP, HCAP, TILE, TILE), (TILE * (OWN_T + N_DEV)) ** -0.5, 0.0625, ((0, 1024),))
    help_col = with_ends(jax.random.randint(splits[4], (DEVS, GROUP, HCAP), 0, GROUP), jax.random.fold_in(splits[4], 1), 0, GROUP - 1).astype(jnp.int32)
    help_count = draw_help_count(jax.random.fold_in(splits[6], 71), 0)
    return dict(basis=basis, own_tiles=own_tiles, own_col=own_col, help_tiles=help_tiles, help_col=help_col, help_count=help_count)


def apply_tiles(ybf, own_tiles, own_col, help_tiles, help_col, help_count):
    blocks = ybf.astype(jnp.float32).reshape(K, N_GRP, N_DEV, TILE)
    far_all = jnp.transpose(blocks, (2, 0, 1, 3))

    def one_group(inputs):
        index, tiles, columns, htiles, hcolumns, hcounts = inputs
        group_blocks = lax.dynamic_index_in_dim(blocks, index, 1, keepdims=False)
        table = jnp.concatenate([jnp.broadcast_to(group_blocks[None], (N_DEV, K, N_DEV, TILE)), far_all], axis=2)
        picked = jax.vmap(lambda tab, col: jnp.take(tab, col, axis=1))(table, columns)
        owned = jnp.einsum("vktc,vtrc->vkr", picked, tiles.astype(jnp.float32))
        helper_cols = jnp.take(group_blocks, hcolumns, axis=1)
        live = jnp.arange(HCAP, dtype=jnp.int32)[None, None, :] < hcounts[:, :, None]
        helper_cols = jnp.where(live[None, :, :, :, None], helper_cols, jnp.float32(0.0))
        helped = jnp.einsum("kupsc,upsrc->pkr", helper_cols, htiles.astype(jnp.float32))
        return owned + helped

    result = lax.map(one_group, (jnp.arange(N_GRP, dtype=jnp.int32),
                                 own_tiles.reshape(N_GRP, N_DEV, OWN_T, TILE, TILE),
                                 own_col.reshape(N_GRP, N_DEV, OWN_T),
                                 help_tiles.reshape(N_GRP, N_DEV, N_DEV, HCAP, TILE, TILE),
                                 help_col.reshape(N_GRP, N_DEV, N_DEV, HCAP),
                                 help_count.reshape(N_GRP, N_DEV, N_DEV)))
    return jnp.transpose(result, (2, 0, 1, 3)).reshape(K, TOTAL_ROWS)


def reference(basis, own_tiles, own_col, help_tiles, help_col, help_count):
    def product(block):
        return apply_tiles(block.astype(jnp.bfloat16), own_tiles, own_col, help_tiles, help_col, help_count)

    first = (product(basis) - 0.5 * basis) / 1.5
    second = 2.0 * (product(first) - 0.5 * first) / 1.5 - basis
    filtered = 2.0 * (product(second) - 0.5 * second) / 1.5 - first
    gram = jnp.dot(filtered, filtered.T, precision=lax.Precision.HIGHEST, preferred_element_type=jnp.float32) / TOTAL_ROWS
    return filtered, gram
```

```python
import functools

import jax
import jax.numpy as jnp
from jax import lax
from jax.experimental import pallas as pl
from jax.experimental.pallas import tpu as pltpu
from jax.sharding import PartitionSpec as P

STRIDE = 4
UNROLL = 4
HEADER = 16
VMEM_LIMIT = 48 * 1024 * 1024


def spread(block, copies, sem, targets):
    copies[...] = jnp.broadcast_to(block.astype(jnp.bfloat16)[None], copies.shape)
    started = []
    for i, target in enumerate(targets):
        copy = pltpu.make_async_copy(copies.at[pl.ds(0, target.shape[0])], target, sem.at[i])
        copy.start()
        started.append(copy)
    for copy in started:
        copy.wait()


def tile_sum(total, count, meta, tile_at, block_at, tiles, blocks, rows):
    def step(j, total):
        left, right = [], []
        for q in range(UNROLL):
            i = j * UNROLL + q
            block = blocks[meta[block_at + i], pl.ds(0, rows)]
            left.append(jnp.where(i < count, block, jnp.zeros_like(block)))
            right.append(tiles[meta[tile_at + i]])
        return total + lax.dot_general(
            jnp.concatenate(left, axis=1),
            jnp.concatenate(right, axis=1),
            (((1,), (1,)), ((), ())),
            preferred_element_type=jnp.float32,
        )

    return lax.fori_loop(0, lax.div(count + (UNROLL - 1), UNROLL), step, total)


def first_kernel(block, header, dev_out, grp_out, copies, sem):
    rows = block.shape[0]
    copies[:, pl.ds(0, rows)] = jnp.broadcast_to(
        block[...].astype(jnp.bfloat16)[None], (copies.shape[0], rows, copies.shape[2])
    )
    copies[:, pl.ds(rows, HEADER)] = header[...]
    one = pltpu.make_async_copy(copies, dev_out, sem.at[0])
    two = pltpu.make_async_copy(
        copies.at[pl.ds(0, grp_out.shape[0]), pl.ds(0, rows)], grp_out, sem.at[1]
    )
    one.start()
    two.start()
    one.wait()
    two.wait()


def near_kernel(places, counts, meta, blocks, own, help_, out):
    total = jnp.zeros(out.shape, jnp.float32)
    rows = out.shape[0]
    total = tile_sum(total, meta[counts], meta, places[0], places[1], own, blocks, rows)
    out[...] = tile_sum(total, meta[counts + 1], meta, places[2], places[3], help_, blocks, rows)


def far_kernel(places, counts, order, meta, z0, z1, z2, z3, own, near, *rest):
    if order == 0:
        now, (nxt, dev_out, grp_out, table, copies, sem) = rest[0], rest[1:]
    elif order == 1:
        now, before, (nxt, dev_out, grp_out, table, copies, sem) = rest[0], rest[1], rest[2:]
    else:
        now, before, (nxt, gram, table, sem) = rest[0], rest[1], rest[2:]
    rows = near.shape[0]
    started = []
    step = z0.shape[0]
    for i, z in enumerate((z0, z1, z2, z3)):
        copy = pltpu.make_async_copy(z, table.at[pl.ds(i * step, step)], sem.at[i])
        copy.start()
        started.append(copy)
    for copy in started:
        copy.wait()
    product = tile_sum(near[...], meta[counts + 2], meta, places[4], places[5], own, table, rows)
    if order == 0:
        value = (product - 0.5 * now[...]) / 1.5
    else:
        value = 2.0 * (product - 0.5 * now[...]) / 1.5 - before[...]
    nxt[...] = value
    if order < 2:
        spread(value, copies, sem, (dev_out, grp_out))
    else:
        gram[...] = lax.dot_general(
            value,
            value,
            (((1,), (1,)), ((), ())),
            precision=lax.Precision.HIGHEST,
            preferred_element_type=jnp.float32,
        )


def packed(live, tile, block):
    n = live.shape[0]
    at = jnp.arange(n, dtype=jnp.int32)
    place = jnp.sum(jnp.where(at[:, None] > at[None, :], live[None, :].astype(jnp.int32), 0), axis=1)
    hit = live[None, :] & (place[None, :] == at[:, None])
    put = lambda v: jnp.sum(jnp.where(hit, v[None, :], 0), axis=1)
    return put(tile), put(block), jnp.sum(live.astype(jnp.int32))


def on_device(basis, own_tiles, own_col, help_tiles, help_col, help_count):
    width, tile = basis.shape
    group_size = lax.axis_size("dev")
    group_count = lax.axis_size("grp")
    slots = help_tiles.shape[2]
    own_n = own_tiles.shape[1]
    help_n = group_size * slots
    runs = group_count // STRIDE
    mine = lax.axis_index("grp")
    bf16, f32, i32 = jnp.bfloat16, jnp.float32, jnp.int32
    vmem = pl.BlockSpec(memory_space=pltpu.VMEM)
    smem = pl.BlockSpec(memory_space=pltpu.SMEM)
    hbm = pl.BlockSpec(memory_space=pltpu.HBM)
    anywhere = pl.BlockSpec(memory_space=pl.ANY)
    params = pltpu.CompilerParams(vmem_limit_bytes=VMEM_LIMIT)
    strided = [[b + STRIDE * a for a in range(runs)] for b in range(STRIDE)]

    header = jnp.concatenate([help_col[0], help_count[0][:, None]], axis=1).astype(bf16)
    header = jnp.pad(header[:, None, :], ((0, 0), (0, HEADER - 1), (0, tile - slots - 1)))
    dev_copies, grp_copies = pl.pallas_call(
        first_kernel,
        out_shape=(
            jax.ShapeDtypeStruct((group_size, width + HEADER, tile), bf16),
            jax.ShapeDtypeStruct((runs, width, tile), bf16),
        ),
        in_specs=[vmem, vmem],
        out_specs=(hbm, hbm),
        scratch_shapes=[
            pltpu.VMEM((group_size, width + HEADER, tile), bf16),
            pltpu.SemaphoreType.DMA((2,)),
        ],
        compiler_params=params,
        name="first_copies",
    )(basis, header)

    def exchange(dev_copies, grp_copies):
        strided_blocks = lax.all_to_all(grp_copies, "grp", 0, 0, axis_index_groups=strided)
        group_blocks = lax.all_to_all(dev_copies, "dev", 0, 0)
        shifted = [strided_blocks]
        for shift in (1, 2, -1):
            shifted.append(
                lax.ppermute(
                    strided_blocks,
                    "grp",
                    [(i, (i - shift) % group_count) for i in range(group_count)],
                )
            )
        return group_blocks, shifted

    group_blocks, shifted = exchange(dev_copies, grp_copies)
    moved = lax.all_to_all(help_tiles[0], "dev", 0, 0).reshape(help_n, tile, tile)

    lent = group_blocks[:, width, : slots + 1].astype(i32)
    help_live = (jnp.arange(slots, dtype=i32)[None, :] < lent[:, slots:]).reshape(help_n)
    help_tile, help_block, help_live_n = packed(
        help_live, jnp.arange(help_n, dtype=i32), lent[:, :slots].reshape(help_n)
    )
    code = own_col[0]
    is_near = code < group_size
    far = code - group_size
    far_block = lax.rem(far - mine + group_count, STRIDE) * runs + lax.div(far, STRIDE)
    own_at = jnp.arange(own_n, dtype=i32)
    near_tile, near_block, near_n = packed(is_near, own_at, code)
    far_tile, far_block, far_n = packed(~is_near, own_at, far_block)
    near_meta = jnp.concatenate(
        [near_tile, near_block, help_tile, help_block, near_n[None], help_live_n[None]]
    )
    far_meta = jnp.concatenate([far_tile, far_block, far_n[None]])
    near_places = (0, own_n, 2 * own_n, 2 * own_n + help_n)
    near_counts = 2 * own_n + 2 * help_n
    far_places = (0, 0, 0, 0, 0, own_n)
    far_counts = 2 * own_n - 2

    block = jax.ShapeDtypeStruct((width, tile), f32)

    def near_part(group_blocks):
        return pl.pallas_call(
            functools.partial(near_kernel, near_places, near_counts),
            out_shape=block,
            in_specs=[smem, vmem, vmem, vmem],
            out_specs=vmem,
            compiler_params=params,
            cost_estimate=pl.CostEstimate(
                flops=2 * width * tile * tile * (own_n + help_n),
                bytes_accessed=2 * tile * tile * (own_n + help_n),
                transcendentals=0,
            ),
            name="near_tiles",
        )(near_meta, group_blocks, own_tiles[0], moved)

    def far_part(order, shifted, near, *states):
        out_shape = [block]
        out_specs = [vmem]
        scratch = [pltpu.VMEM((group_count, width, tile), bf16)]
        if order < 2:
            out_shape.append(jax.ShapeDtypeStruct((group_size, width, tile), bf16))
            out_shape.append(jax.ShapeDtypeStruct((runs, width, tile), bf16))
            out_specs += [hbm, hbm]
            scratch.append(pltpu.VMEM((group_size, width, tile), bf16))
        else:
            out_shape.append(jax.ShapeDtypeStruct((width, width), f32))
            out_specs.append(vmem)
        scratch.append(pltpu.SemaphoreType.DMA((STRIDE,)))
        return pl.pallas_call(
            functools.partial(far_kernel, far_places, far_counts, order),
            out_shape=tuple(out_shape),
            in_specs=[smem] + [anywhere] * STRIDE + [vmem] * (2 + len(states)),
            out_specs=tuple(out_specs),
            scratch_shapes=scratch,
            compiler_params=params,
            name="far_tiles",
        )(far_meta, *shifted, own_tiles[0], near, *states)

    near = near_part(group_blocks)
    first, dev_copies, grp_copies = far_part(0, shifted, near, basis)
    group_blocks, shifted = exchange(dev_copies, grp_copies)
    near = near_part(group_blocks)
    second, dev_copies, grp_copies = far_part(1, shifted, near, first, basis)
    group_blocks, shifted = exchange(dev_copies, grp_copies)
    near = near_part(group_blocks)
    filtered, local_gram = far_part(2, shifted, near, second, first)

    chunk = width // group_size
    chunks = lax.all_to_all(local_gram.reshape(group_size, chunk, width), "dev", 0, 0)
    part = jnp.sum(chunks, axis=0)
    parts = lax.all_to_all(
        jnp.broadcast_to(part[None], (group_count, chunk, width)), "grp", 0, 0
    )
    part = jnp.sum(parts, axis=0)
    whole = lax.all_to_all(jnp.broadcast_to(part[None], (group_size, chunk, width)), "dev", 0, 0)
    gram = whole.reshape(width, width) / (tile * group_size * group_count)
    return filtered, gram


def solution(mesh):
    in_specs = (
        P(None, ("grp", "dev")),
        P(("grp", "dev"), None, None, None),
        P(("grp", "dev"), None),
        P(("grp", "dev"), None, None, None, None),
        P(("grp", "dev"), None, None),
        P(("grp", "dev"), None),
    )
    out_specs = (P(None, ("grp", "dev")), P())
    return jax.shard_map(
        on_device, mesh=mesh, in_specs=in_specs, out_specs=out_specs, check_vma=False
    )
```

```python
import functools

import jax
import jax.numpy as jnp
from jax import lax
from jax.experimental import pallas as pl
from jax.experimental.pallas import tpu as pltpu
from jax.sharding import PartitionSpec as P

STRIDE = 4
SHIFTS = {2: (1, -1), 4: (1, 2, -1)}[STRIDE]
UNROLL = 8
HEADER = 16
SHARED_VMEM = 32 * 1024 * 1024
WHOLE_VMEM = 60 * 1024 * 1024
BF16, F32, I32 = jnp.bfloat16, jnp.float32, jnp.int32


def add_tiles(total, blocks, tiles):
    return total + lax.dot_general(
        jnp.concatenate(blocks, axis=1),
        jnp.concatenate(tiles, axis=1),
        (((1,), (1,)), ((), ())),
        preferred_element_type=F32,
    )


def masked(block, live):
    return jnp.where(live, block, jnp.zeros_like(block))


def first_kernel(col, count, block, help_, packed, rounded, copies, sem):
    group, tile_rows, tile = help_.shape
    rows, slots = block.shape[0], col.shape[2]
    moved = pltpu.make_async_copy(help_, packed.at[:, pl.ds(0, tile_rows)], sem.at[0])
    moved.start()
    value = block[...].astype(BF16)
    rounded[...] = value
    copies[:, pl.ds(0, rows)] = jnp.broadcast_to(value[None], (group, rows, tile))
    lane = lax.broadcasted_iota(I32, (HEADER, tile), 1)

    def fill(p, carry):
        codes = jnp.full((HEADER, tile), -1, I32)
        for s in range(slots):
            codes = jnp.where(lane == s, jnp.where(s < count[0, p], col[0, p, s], -1), codes)
        copies[p, pl.ds(rows, HEADER)] = codes.astype(F32).astype(BF16)
        return carry

    lax.fori_loop(0, group, fill, 0)
    rest = pltpu.make_async_copy(
        copies, packed.at[:, pl.ds(tile_rows, rows + HEADER)], sem.at[1]
    )
    rest.start()
    moved.wait()
    rest.wait()


def near_kernel(at, code, lent, group_blocks, tiles, packed, out, blocks, own, helped, sem):
    group, tile_rows, tile = helped.shape
    rows = out.shape[0]
    slots = tile_rows // tile
    own_n = own.shape[0]
    copies = [
        pltpu.make_async_copy(group_blocks.at[:, pl.ds(at, rows)], blocks, sem.at[0]),
        pltpu.make_async_copy(tiles, own, sem.at[1]),
        pltpu.make_async_copy(packed.at[:, pl.ds(0, tile_rows)], helped, sem.at[2]),
    ]
    for copy in copies:
        copy.start()
    total = jnp.zeros(out.shape, F32)

    def pick(block, live):
        return masked(blocks[jnp.where(live, block, 0)], live)

    copies[0].wait()
    copies[1].wait()
    for t in range(0, own_n, UNROLL):
        codes = [code[0, i] for i in range(t, t + UNROLL)]
        total = add_tiles(
            total,
            [pick(c, c < group) for c in codes],
            [own[i] for i in range(t, t + UNROLL)],
        )
    copies[2].wait()
    for t in range(0, group * slots, UNROLL):
        places = [(i // slots, i % slots) for i in range(t, t + UNROLL)]
        codes = [lent[u, s] for u, s in places]
        total = add_tiles(
            total,
            [pick(c, c >= 0) for c in codes],
            [helped[u, pl.ds(s * tile, tile)] for u, s in places],
        )
    out[...] = total


def far_kernel(order, group, pieces, mine, code, *refs):
    parts, (tiles, near), refs = refs[:pieces], refs[pieces : pieces + 2], refs[pieces + 2 :]
    if order == 0:
        now, (nxt, dev_out, grp_out, own, table, copies, sem) = refs[0], refs[1:]
    elif order == 1:
        now, before, (nxt, dev_out, grp_out, own, table, copies, sem) = refs[0], refs[1], refs[2:]
    else:
        now, before, (nxt, gram, own, table, sem) = refs[0], refs[1], refs[2:]
    copy = pltpu.make_async_copy(tiles, own, sem.at[4])
    copy.start()
    started, at = [copy], 0
    for i, part in enumerate(parts):
        copy = pltpu.make_async_copy(part, table.at[pl.ds(at, part.shape[0])], sem.at[i])
        copy.start()
        started.append(copy)
        at += part.shape[0]
    for copy in started:
        copy.wait()
    runs = table.shape[0] // STRIDE
    product = near[...]
    for t in range(0, own.shape[0], UNROLL):
        blocks = []
        for i in range(t, t + UNROLL):
            live = code[0, i] >= group
            far = jnp.where(live, code[0, i] - group, 0)
            place = lax.rem(far - mine[0] + table.shape[0], STRIDE) * runs + lax.div(far, STRIDE)
            blocks.append(masked(table[place], live))
        product = add_tiles(product, blocks, [own[i] for i in range(t, t + UNROLL)])
    if order == 0:
        value = (product - 0.5 * now[...]) / 1.5
    else:
        value = 2.0 * (product - 0.5 * now[...]) / 1.5 - before[...]
    nxt[...] = value
    if order < 2:
        copies[...] = jnp.broadcast_to(value.astype(BF16)[None], copies.shape)
        one = pltpu.make_async_copy(copies, dev_out, sem.at[0])
        two = pltpu.make_async_copy(copies.at[pl.ds(0, grp_out.shape[0])], grp_out, sem.at[1])
        two.start()
        one.start()
        two.wait()
        one.wait()
    else:
        gram[...] = lax.dot_general(
            value,
            value,
            (((1,), (1,)), ((), ())),
            precision=lax.Precision.HIGHEST,
            preferred_element_type=F32,
        )


def on_device(basis, own_tiles, own_col, help_tiles, help_col, help_count):
    width, tile = basis.shape
    group_size = lax.axis_size("dev")
    group_count = lax.axis_size("grp")
    slots = help_tiles.shape[2]
    own_n = own_tiles.shape[1]
    runs = group_count // STRIDE
    mine = lax.axis_index("grp").astype(I32)[None]
    vmem = pl.BlockSpec(memory_space=pltpu.VMEM)
    smem = pl.BlockSpec(memory_space=pltpu.SMEM)
    hbm = pl.BlockSpec(memory_space=pltpu.HBM)
    anywhere = pl.BlockSpec(memory_space=pl.ANY)
    whole = pltpu.CompilerParams(vmem_limit_bytes=WHOLE_VMEM)
    shared = pltpu.CompilerParams(vmem_limit_bytes=SHARED_VMEM)
    strided = [[b + STRIDE * a for a in range(runs)] for b in range(STRIDE)]
    block = jax.ShapeDtypeStruct((width, tile), F32)
    tile_rows = slots * tile

    packed, rounded = pl.pallas_call(
        first_kernel,
        out_shape=(
            jax.ShapeDtypeStruct((group_size, tile_rows + width + HEADER, tile), BF16),
            jax.ShapeDtypeStruct((width, tile), BF16),
        ),
        in_specs=[smem, smem, vmem, anywhere],
        out_specs=(hbm, vmem),
        scratch_shapes=[
            pltpu.VMEM((group_size, width + HEADER, tile), BF16),
            pltpu.SemaphoreType.DMA((2,)),
        ],
        compiler_params=whole,
        name="first_copies",
    )(help_col, help_count, basis, help_tiles[0].reshape(group_size, tile_rows, tile))

    def from_neighbours(strided_blocks):
        shifted = [strided_blocks]
        for n, shift in enumerate(SHIFTS):
            piece = strided_blocks
            if STRIDE == 2:
                piece = strided_blocks[n * (runs // 2) : (n + 1) * (runs // 2)]
            pairs = [(i, (i - shift) % group_count) for i in range(group_count)]
            shifted.append(lax.ppermute(piece, "grp", pairs))
        return shifted

    def near_part(at, blocks):
        return pl.pallas_call(
            functools.partial(near_kernel, at),
            out_shape=block,
            in_specs=[smem, smem, anywhere, anywhere, anywhere],
            out_specs=vmem,
            scratch_shapes=[
                pltpu.VMEM((group_size, width, tile), BF16),
                pltpu.VMEM((own_n, tile, tile), BF16),
                pltpu.VMEM((group_size, tile_rows, tile), BF16),
                pltpu.SemaphoreType.DMA((3,)),
            ],
            compiler_params=shared,
            cost_estimate=pl.CostEstimate(
                flops=2 * width * tile * tile * (own_n + group_size * slots),
                bytes_accessed=2 * tile * tile * (own_n + group_size * slots),
                transcendentals=0,
            ),
            name="near_tiles",
        )(own_col, lent, blocks, own_tiles[0], packed)

    def far_part(order, shifted, near, *states):
        out_shape = [block]
        out_specs = [vmem]
        scratch = [
            pltpu.VMEM((own_n, tile, tile), BF16),
            pltpu.VMEM((group_count, width, tile), BF16),
        ]
        if order < 2:
            out_shape.append(jax.ShapeDtypeStruct((group_size, width, tile), BF16))
            out_shape.append(jax.ShapeDtypeStruct((runs, width, tile), BF16))
            out_specs += [hbm, hbm]
            scratch.append(pltpu.VMEM((group_size, width, tile), BF16))
        else:
            out_shape.append(jax.ShapeDtypeStruct((width, width), F32))
            out_specs.append(vmem)
        scratch.append(pltpu.SemaphoreType.DMA((5,)))
        return pl.pallas_call(
            functools.partial(far_kernel, order, group_size, len(shifted)),
            out_shape=tuple(out_shape),
            in_specs=[smem, smem] + [anywhere] * (len(shifted) + 1) + [vmem] * (1 + len(states)),
            out_specs=tuple(out_specs),
            scratch_shapes=scratch,
            compiler_params=whole,
            name="far_tiles",
        )(mine, own_col, *shifted, own_tiles[0], near, *states)

    packed = lax.all_to_all(packed, "dev", 0, 0)
    strided_blocks = lax.all_gather(rounded, "grp", axis=0, axis_index_groups=strided)
    shifted = from_neighbours(strided_blocks)
    lent = packed[:, tile_rows + width, :slots].astype(I32)
    near = near_part(tile_rows, packed)
    first, dev_copies, grp_copies = far_part(0, shifted, near, basis)

    def exchange(dev_copies, grp_copies):
        strided_blocks = lax.all_to_all(grp_copies, "grp", 0, 0, axis_index_groups=strided)
        group_blocks = lax.all_to_all(dev_copies, "dev", 0, 0)
        return group_blocks, from_neighbours(strided_blocks)

    group_blocks, shifted = exchange(dev_copies, grp_copies)
    near = near_part(0, group_blocks)
    second, dev_copies, grp_copies = far_part(1, shifted, near, first, basis)
    group_blocks, shifted = exchange(dev_copies, grp_copies)
    near = near_part(0, group_blocks)
    filtered, local_gram = far_part(2, shifted, near, second, first)

    chunk = width // group_size
    chunks = lax.all_to_all(local_gram.reshape(group_size, chunk, width), "dev", 0, 0)
    part = jnp.sum(chunks, axis=0)
    parts = lax.all_to_all(
        jnp.broadcast_to(part[None], (group_count, chunk, width)), "grp", 0, 0
    )
    part = jnp.sum(parts, axis=0)
    full = lax.all_to_all(jnp.broadcast_to(part[None], (group_size, chunk, width)), "dev", 0, 0)
    gram = full.reshape(width, width) / (tile * group_size * group_count)
    return filtered, gram


def solution(mesh):
    in_specs = (
        P(None, ("grp", "dev")),
        P(("grp", "dev"), None, None, None),
        P(("grp", "dev"), None),
        P(("grp", "dev"), None, None, None, None),
        P(("grp", "dev"), None, None),
        P(("grp", "dev"), None),
    )
    out_specs = (P(None, ("grp", "dev")), P())
    return jax.shard_map(
        on_device, mesh=mesh, in_specs=in_specs, out_specs=out_specs, check_vma=False
    )
```

```python
import functools

import jax
import jax.numpy as jnp
from jax import lax
from jax.experimental import pallas as pl
from jax.experimental.pallas import tpu as pltpu
from jax.sharding import PartitionSpec as P

STRIDE = 4
SHIFTS = {2: (1, -1), 4: (1, 2, -1)}[STRIDE]
UNROLL = 8
HEADER = 16
CUTS = 4
SHARED_VMEM = 32 * 1024 * 1024
WHOLE_VMEM = 60 * 1024 * 1024
BF16, F32, I32 = jnp.bfloat16, jnp.float32, jnp.int32


def add_tiles(total, blocks, tiles):
    return total + lax.dot_general(
        jnp.concatenate(blocks, axis=1),
        jnp.concatenate(tiles, axis=1),
        (((1,), (1,)), ((), ())),
        preferred_element_type=F32,
    )


def masked(block, live):
    return jnp.where(live, block, jnp.zeros_like(block))


def start_all(pairs, sem, first=0):
    copies = [
        pltpu.make_async_copy(source, target, sem.at[first + i])
        for i, (source, target) in enumerate(pairs)
    ]
    for copy in copies:
        copy.start()
    return copies


def cut(source, target, parts):
    step = target.shape[0] // parts
    return [
        (source.at[pl.ds(i * step, step)], target.at[pl.ds(i * step, step)]) for i in range(parts)
    ]


def first_kernel(col, count, basis, help_, packed, rounded, block, copies, sem):
    group, tile_rows, tile = help_.shape
    rows, slots = basis.shape[0], col.shape[2]
    begun = start_all(
        [(basis, block)]
        + [(a, b) for a, b in cut(help_, copies.at[:, pl.ds(0, tile_rows)], CUTS)],
        sem,
    )
    lane = lax.broadcasted_iota(I32, (HEADER, tile), 1)

    def fill(p, carry):
        codes = jnp.full((HEADER, tile), -1, I32)
        for s in range(slots):
            codes = jnp.where(lane == s, jnp.where(s < count[0, p], col[0, p, s], -1), codes)
        copies[p, pl.ds(tile_rows + rows, HEADER)] = codes.astype(F32).astype(BF16)
        return carry

    lax.fori_loop(0, group, fill, 0)
    begun[0].wait()
    value = block[...].astype(BF16)
    rounded[...] = value
    copies[:, pl.ds(tile_rows, rows)] = jnp.broadcast_to(value[None], (group, rows, tile))
    ended = []
    for i, pair in enumerate(cut(copies, packed, CUTS)):
        begun[1 + i].wait()
        ended += start_all([pair], sem, 1 + CUTS + i)
    for copy in ended:
        copy.wait()


def near_kernel(at, code, lent, group_blocks, tiles, packed, out, blocks, own, helped, sem):
    group, tile_rows, tile = helped.shape
    rows = out.shape[0]
    slots = tile_rows // tile
    own_n = own.shape[0]
    first = start_all(
        [(group_blocks.at[:, pl.ds(at, rows)], blocks)] + cut(tiles, own, CUTS), sem
    )
    second = start_all(cut(packed.at[:, pl.ds(0, tile_rows)], helped, CUTS), sem, 1 + CUTS)
    total = jnp.zeros(out.shape, F32)

    def pick(block, live):
        return masked(blocks[jnp.where(live, block, 0)], live)

    for copy in first:
        copy.wait()
    for t in range(0, own_n, UNROLL):
        codes = [code[0, i] for i in range(t, t + UNROLL)]
        total = add_tiles(
            total,
            [pick(c, c < group) for c in codes],
            [own[i] for i in range(t, t + UNROLL)],
        )
    for copy in second:
        copy.wait()
    for t in range(0, group * slots, UNROLL):
        places = [(i // slots, i % slots) for i in range(t, t + UNROLL)]
        codes = [lent[u, s] for u, s in places]
        total = add_tiles(
            total,
            [pick(c, c >= 0) for c in codes],
            [helped[u, pl.ds(s * tile, tile)] for u, s in places],
        )
    out[...] = total


def far_kernel(order, group, pieces, mine, code, *refs):
    parts, tiles, refs = refs[:pieces], refs[pieces], refs[pieces + 1 :]
    n = 3 if order else 2
    states, refs = refs[:n], refs[n:]
    if order < 2:
        nxt, dev_out, grp_out, own, table, held, value_at, copies, sem = refs
    else:
        nxt, gram, own, table, held, value_at, sem = refs
    pairs, at = [], 0
    for part in parts:
        pairs.append((part, table.at[pl.ds(at, part.shape[0])]))
        at += part.shape[0]
    pairs += cut(tiles, own, CUTS)
    pairs += [(state, held.at[i]) for i, state in enumerate(states)]
    for copy in start_all(pairs, sem):
        copy.wait()
    runs = table.shape[0] // STRIDE
    product = held[0]
    for t in range(0, own.shape[0], UNROLL):
        blocks = []
        for i in range(t, t + UNROLL):
            live = code[0, i] >= group
            far = jnp.where(live, code[0, i] - group, 0)
            place = lax.rem(far - mine[0] + table.shape[0], STRIDE) * runs + lax.div(far, STRIDE)
            blocks.append(masked(table[place], live))
        product = add_tiles(product, blocks, [own[i] for i in range(t, t + UNROLL)])
    if order == 0:
        value = (product - 0.5 * held[1]) / 1.5
    else:
        value = 2.0 * (product - 0.5 * held[1]) / 1.5 - held[2]
    value_at[...] = value
    pairs = [(value_at, nxt)]
    if order < 2:
        copies[...] = jnp.broadcast_to(value.astype(BF16)[None], copies.shape)
        pairs.append((copies.at[pl.ds(0, grp_out.shape[0])], grp_out))
        pairs += cut(copies, dev_out, CUTS)
    ended = start_all(pairs, sem)
    if order == 2:
        whole = lax.dot_general(
            value,
            value,
            (((1,), (1,)), ((), ())),
            precision=lax.Precision.HIGHEST,
            preferred_element_type=F32,
        )
        n = gram.shape[0]
        rows = [whole[i : i + n] for i in range(0, whole.shape[0], n)]
        gram[...] = jnp.concatenate(rows, axis=1).reshape(gram.shape)
    for copy in ended:
        copy.wait()


def sum_kernel(parts, out):
    out[...] = jnp.broadcast_to(jnp.sum(parts[...], axis=0, keepdims=True), out.shape)


def last_kernel(nodes, parts, out):
    whole = parts[...].reshape(parts.shape[0], parts.shape[2]) / nodes
    n, width = whole.shape[0], out.shape[1]
    for i in range(out.shape[0] // n):
        out[pl.ds(i * n, n)] = whole[:, i * width : (i + 1) * width]


def on_device(basis, own_tiles, own_col, help_tiles, help_col, help_count):
    width, tile = basis.shape
    group_size = lax.axis_size("dev")
    group_count = lax.axis_size("grp")
    slots = help_tiles.shape[2]
    own_n = own_tiles.shape[1]
    runs = group_count // STRIDE
    mine = lax.axis_index("grp").astype(I32)[None]
    vmem = pl.BlockSpec(memory_space=pltpu.VMEM)
    smem = pl.BlockSpec(memory_space=pltpu.SMEM)
    hbm = pl.BlockSpec(memory_space=pltpu.HBM)
    anywhere = pl.BlockSpec(memory_space=pl.ANY)
    whole = pltpu.CompilerParams(vmem_limit_bytes=WHOLE_VMEM)
    shared = pltpu.CompilerParams(vmem_limit_bytes=SHARED_VMEM)
    strided = [[b + STRIDE * a for a in range(runs)] for b in range(STRIDE)]
    block = jax.ShapeDtypeStruct((width, tile), F32)
    tile_rows = slots * tile

    packed, rounded = pl.pallas_call(
        first_kernel,
        out_shape=(
            jax.ShapeDtypeStruct((group_size, tile_rows + width + HEADER, tile), BF16),
            jax.ShapeDtypeStruct((width, tile), BF16),
        ),
        in_specs=[smem, smem, anywhere, anywhere],
        out_specs=(hbm, vmem),
        scratch_shapes=[
            pltpu.VMEM((width, tile), F32),
            pltpu.VMEM((group_size, tile_rows + width + HEADER, tile), BF16),
            pltpu.SemaphoreType.DMA((1 + 2 * CUTS,)),
        ],
        compiler_params=whole,
        name="first_copies",
    )(help_col, help_count, basis, help_tiles[0].reshape(group_size, tile_rows, tile))

    def from_neighbours(strided_blocks):
        shifted = [strided_blocks]
        for n, shift in enumerate(SHIFTS):
            piece = strided_blocks
            if STRIDE == 2:
                piece = strided_blocks[n * (runs // 2) : (n + 1) * (runs // 2)]
            pairs = [(i, (i - shift) % group_count) for i in range(group_count)]
            shifted.append(lax.ppermute(piece, "grp", pairs))
        return shifted

    def near_part(at, blocks):
        return pl.pallas_call(
            functools.partial(near_kernel, at),
            out_shape=block,
            in_specs=[smem, smem, anywhere, anywhere, anywhere],
            out_specs=vmem,
            scratch_shapes=[
                pltpu.VMEM((group_size, width, tile), BF16),
                pltpu.VMEM((own_n, tile, tile), BF16),
                pltpu.VMEM((group_size, tile_rows, tile), BF16),
                pltpu.SemaphoreType.DMA((1 + 2 * CUTS,)),
            ],
            compiler_params=shared,
            cost_estimate=pl.CostEstimate(
                flops=2 * width * tile * tile * (own_n + group_size * slots),
                bytes_accessed=2 * tile * tile * (own_n + group_size * slots),
                transcendentals=0,
            ),
            name="near_tiles",
        )(own_col, lent, blocks, own_tiles[0], packed)

    chunk_width = width * width // group_size

    def far_part(order, shifted, *states):
        out_shape, out_specs = [block], [hbm]
        scratch = [
            pltpu.VMEM((own_n, tile, tile), BF16),
            pltpu.VMEM((group_count, width, tile), BF16),
            pltpu.VMEM((len(states), width, tile), F32),
            pltpu.VMEM((width, tile), F32),
        ]
        if order < 2:
            out_shape.append(jax.ShapeDtypeStruct((group_size, width, tile), BF16))
            out_shape.append(jax.ShapeDtypeStruct((runs, width, tile), BF16))
            out_specs += [hbm, hbm]
            scratch.append(pltpu.VMEM((group_size, width, tile), BF16))
        else:
            out_shape.append(jax.ShapeDtypeStruct((group_size, 1, chunk_width), F32))
            out_specs.append(vmem)
        scratch.append(pltpu.SemaphoreType.DMA((len(shifted) + CUTS + len(states),)))
        return pl.pallas_call(
            functools.partial(far_kernel, order, group_size, len(shifted)),
            out_shape=tuple(out_shape),
            in_specs=[smem, smem] + [anywhere] * (len(shifted) + 1 + len(states)),
            out_specs=tuple(out_specs),
            scratch_shapes=scratch,
            compiler_params=whole,
            name="far_tiles",
        )(mine, own_col, *shifted, own_tiles[0], *states)

    packed = lax.all_to_all(packed, "dev", 0, 0)
    strided_blocks = lax.all_gather(rounded, "grp", axis=0, axis_index_groups=strided)
    shifted = from_neighbours(strided_blocks)
    lent = packed[:, tile_rows + width, :slots].astype(I32)
    near = near_part(tile_rows, packed)
    first, dev_copies, grp_copies = far_part(0, shifted, near, basis)

    def exchange(dev_copies, grp_copies):
        strided_blocks = lax.all_to_all(grp_copies, "grp", 0, 0, axis_index_groups=strided)
        group_blocks = lax.all_to_all(dev_copies, "dev", 0, 0)
        return group_blocks, from_neighbours(strided_blocks)

    group_blocks, shifted = exchange(dev_copies, grp_copies)
    near = near_part(0, group_blocks)
    second, dev_copies, grp_copies = far_part(1, shifted, near, first, basis)
    group_blocks, shifted = exchange(dev_copies, grp_copies)
    near = near_part(0, group_blocks)
    filtered, local_gram = far_part(2, shifted, near, second, first)

    def summed(parts, copies):
        return pl.pallas_call(
            sum_kernel,
            out_shape=jax.ShapeDtypeStruct((copies, 1, chunk_width), F32),
            in_specs=[vmem],
            out_specs=vmem,
            compiler_params=shared,
            name="sum_chunks",
        )(parts)

    parts = summed(lax.all_to_all(local_gram, "dev", 0, 0), group_count)
    parts = summed(lax.all_to_all(parts, "grp", 0, 0), group_size)
    parts = lax.all_to_all(parts, "dev", 0, 0)
    gram = pl.pallas_call(
        functools.partial(last_kernel, tile * group_size * group_count),
        out_shape=jax.ShapeDtypeStruct((width, width), F32),
        in_specs=[vmem],
        out_specs=vmem,
        compiler_params=shared,
        name="last_gram",
    )(parts)
    return filtered, gram


def solution(mesh):
    in_specs = (
        P(None, ("grp", "dev")),
        P(("grp", "dev"), None, None, None),
        P(("grp", "dev"), None),
        P(("grp", "dev"), None, None, None, None),
        P(("grp", "dev"), None, None),
        P(("grp", "dev"), None),
    )
    out_specs = (P(None, ("grp", "dev")), P())
    return jax.shard_map(
        on_device, mesh=mesh, in_specs=in_specs, out_specs=out_specs, check_vma=False
    )
```

```python
import functools

import jax
import jax.numpy as jnp
from jax import lax
from jax.experimental import pallas as pl
from jax.experimental.pallas import tpu as pltpu
from jax.sharding import PartitionSpec as P

STRIDE = 4
SHIFTS = {2: (1, -1), 4: (1, 2, -1)}[STRIDE]
UNROLL = 8
HEADER = 16
CUTS = 8
SHARED_VMEM = 16 * 1024 * 1024
WHOLE_VMEM = 60 * 1024 * 1024
BF16, F32, I32 = jnp.bfloat16, jnp.float32, jnp.int32


def add_tiles(total, blocks, tiles):
    return total + lax.dot_general(
        jnp.concatenate(blocks, axis=1),
        jnp.concatenate(tiles, axis=1),
        (((1,), (1,)), ((), ())),
        preferred_element_type=F32,
    )


def masked(block, live):
    return jnp.where(live, block, jnp.zeros_like(block))


def start_all(pairs, sem, first=0):
    copies = [
        pltpu.make_async_copy(source, target, sem.at[first + i])
        for i, (source, target) in enumerate(pairs)
    ]
    for copy in copies:
        copy.start()
    return copies


def cut(source, target, parts):
    step = max(1, target.shape[0] // parts)
    parts = target.shape[0] // step
    return [
        (source.at[pl.ds(i * step, step)], target.at[pl.ds(i * step, step)]) for i in range(parts)
    ]


def first_kernel(col, count, basis, help_, packed, rounded, block, copies, sem):
    group, tile_rows, tile = help_.shape
    rows, slots = basis.shape[0], col.shape[0]
    begun = start_all(
        [(basis, block)]
        + [(a, b) for a, b in cut(help_, copies.at[:, pl.ds(0, tile_rows)], CUTS)],
        sem,
    )
    lane = lax.broadcasted_iota(I32, (HEADER, tile), 1)

    def fill(p, carry):
        codes = jnp.full((HEADER, tile), -1, I32)
        for s in range(slots):
            codes = jnp.where(lane == s, jnp.where(s < count[0, p], col[s, p], -1), codes)
        copies[p, pl.ds(tile_rows + rows, HEADER)] = codes.astype(F32).astype(BF16)
        return carry

    lax.fori_loop(0, group, fill, 0)
    begun[0].wait()
    value = block[...].astype(BF16)
    rounded[...] = value
    copies[:, pl.ds(tile_rows, rows)] = jnp.broadcast_to(value[None], (group, rows, tile))
    ended = []
    for i, pair in enumerate(cut(copies, packed, CUTS)):
        begun[1 + i].wait()
        ended += start_all([pair], sem, 1 + CUTS + i)
    for copy in ended:
        copy.wait()


def near_kernel(at, code, lent, blocks, own, packed, out):
    group = packed.shape[0]
    rows, tile = out.shape
    slots = lent.shape[1]
    own_n = own.shape[0]
    total = jnp.zeros(out.shape, F32)

    def pick(c, live):
        return masked(blocks[jnp.where(live, c, 0), pl.ds(at, rows)], live)

    for t in range(0, own_n, UNROLL):
        codes = [code[0, i] for i in range(t, t + UNROLL)]
        total = add_tiles(
            total,
            [pick(c, c < group) for c in codes],
            [own[i] for i in range(t, t + UNROLL)],
        )
    for t in range(0, group * slots, UNROLL):
        places = [(i // slots, i % slots) for i in range(t, t + UNROLL)]
        codes = [lent[u, s] for u, s in places]
        total = add_tiles(
            total,
            [pick(c, c >= 0) for c in codes],
            [packed[u, pl.ds(s * tile, tile)] for u, s in places],
        )
    out[...] = total


def far_kernel(order, group, pieces, mine, code, *refs):
    parts, own, refs = refs[:pieces], refs[pieces], refs[pieces + 1 :]
    if order == 0:
        near, now, nxt, dev_out, grp_out = refs
    elif order == 1:
        near, now, before, nxt, dev_out, grp_out = refs
    else:
        near, now, before, nxt, gram = refs
    total_runs = parts[0].shape[0]

    def pick(c):
        live = c >= group
        far = jnp.where(live, c - group, 0)
        turn = lax.rem(far - mine[0] + STRIDE * total_runs, STRIDE)
        run = lax.div(far, STRIDE)
        found = masked(parts[0][run], live & (turn == 0))
        for i in range(1, STRIDE):
            found = jnp.where(live & (turn == i), parts[i][run], found)
        return found

    product = near[...]
    for t in range(0, own.shape[0], UNROLL):
        codes = [code[0, i] for i in range(t, t + UNROLL)]
        product = add_tiles(
            product, [pick(c) for c in codes], [own[i] for i in range(t, t + UNROLL)]
        )
    if order == 0:
        value = (product - 0.5 * now[...]) / 1.5
    else:
        value = 2.0 * (product - 0.5 * now[...]) / 1.5 - before[...]
    nxt[...] = value
    if order < 2:
        rounded = value.astype(BF16)[None]
        dev_out[...] = jnp.broadcast_to(rounded, dev_out.shape)
        grp_out[...] = jnp.broadcast_to(rounded, grp_out.shape)
    else:
        whole = lax.dot_general(
            value,
            value,
            (((1,), (1,)), ((), ())),
            precision=lax.Precision.HIGHEST,
            preferred_element_type=F32,
        )
        n = gram.shape[0]
        rows = [whole[i : i + n] for i in range(0, whole.shape[0], n)]
        gram[...] = jnp.concatenate(rows, axis=1).reshape(gram.shape)


def sum_kernel(parts, out):
    out[...] = jnp.broadcast_to(jnp.sum(parts[...], axis=0, keepdims=True), out.shape)


def last_kernel(nodes, parts, out):
    whole = parts[...].reshape(parts.shape[0], parts.shape[2]) / nodes
    n, width = whole.shape[0], out.shape[1]
    for i in range(out.shape[0] // n):
        out[pl.ds(i * n, n)] = whole[:, i * width : (i + 1) * width]


def on_device(basis, own_tiles, own_col, help_tiles, help_col, help_count):
    width, tile = basis.shape
    group_size = lax.axis_size("dev")
    group_count = lax.axis_size("grp")
    slots = help_tiles.shape[2]
    own_n = own_tiles.shape[1]
    runs = group_count // STRIDE
    mine = lax.axis_index("grp").astype(I32)[None]
    vmem = pl.BlockSpec(memory_space=pltpu.VMEM)
    smem = pl.BlockSpec(memory_space=pltpu.SMEM)
    hbm = pl.BlockSpec(memory_space=pltpu.HBM)
    anywhere = pl.BlockSpec(memory_space=pl.ANY)
    whole = pltpu.CompilerParams(vmem_limit_bytes=WHOLE_VMEM)
    shared = pltpu.CompilerParams(vmem_limit_bytes=SHARED_VMEM)
    strided = [[b + STRIDE * a for a in range(runs)] for b in range(STRIDE)]
    block = jax.ShapeDtypeStruct((width, tile), F32)
    tile_rows = slots * tile

    packed, rounded = pl.pallas_call(
        first_kernel,
        out_shape=(
            jax.ShapeDtypeStruct((group_size, tile_rows + width + HEADER, tile), BF16),
            jax.ShapeDtypeStruct((width, tile), BF16),
        ),
        in_specs=[smem, smem, anywhere, anywhere],
        out_specs=(hbm, vmem),
        scratch_shapes=[
            pltpu.VMEM((width, tile), F32),
            pltpu.VMEM((group_size, tile_rows + width + HEADER, tile), BF16),
            pltpu.SemaphoreType.DMA((1 + 2 * CUTS,)),
        ],
        compiler_params=whole,
        name="first_copies",
    )(help_col[0].T, help_count, basis, help_tiles[0].reshape(group_size, tile_rows, tile))

    def from_neighbours(strided_blocks):
        shifted = [strided_blocks]
        for n, shift in enumerate(SHIFTS):
            piece = strided_blocks
            if STRIDE == 2:
                piece = strided_blocks[n * (runs // 2) : (n + 1) * (runs // 2)]
            pairs = [(i, (i - shift) % group_count) for i in range(group_count)]
            shifted.append(lax.ppermute(piece, "grp", pairs))
        return shifted

    def near_part(at, blocks):
        return pl.pallas_call(
            functools.partial(near_kernel, at),
            out_shape=block,
            in_specs=[smem, smem, vmem, vmem, vmem],
            out_specs=vmem,
            compiler_params=shared,
            cost_estimate=pl.CostEstimate(
                flops=2 * width * tile * tile * (own_n + group_size * slots),
                bytes_accessed=2 * tile * tile * (own_n + group_size * slots),
                transcendentals=0,
            ),
            name="near_tiles",
        )(own_col, lent, blocks, own_tiles[0], packed)

    chunk_width = width * width // group_size

    def far_part(order, shifted, *states):
        out_shape = [block]
        if order < 2:
            out_shape.append(jax.ShapeDtypeStruct((group_size, width, tile), BF16))
            out_shape.append(jax.ShapeDtypeStruct((runs, width, tile), BF16))
        else:
            out_shape.append(jax.ShapeDtypeStruct((group_size, 1, chunk_width), F32))
        return pl.pallas_call(
            functools.partial(far_kernel, order, group_size, len(shifted)),
            out_shape=tuple(out_shape),
            in_specs=[smem, smem] + [vmem] * (len(shifted) + 1 + len(states)),
            out_specs=(vmem,) * len(out_shape),
            compiler_params=shared,
            name="far_tiles",
        )(mine, own_col, *shifted, own_tiles[0], *states)

    packed = lax.all_to_all(packed, "dev", 0, 0)
    strided_blocks = lax.all_gather(rounded, "grp", axis=0, axis_index_groups=strided)
    shifted = from_neighbours(strided_blocks)
    lent = packed[:, tile_rows + width, :slots].astype(I32)
    near = near_part(tile_rows, packed)
    first, dev_copies, grp_copies = far_part(0, shifted, near, basis)

    def exchange(dev_copies, grp_copies):
        strided_blocks = lax.all_to_all(grp_copies, "grp", 0, 0, axis_index_groups=strided)
        group_blocks = lax.all_to_all(dev_copies, "dev", 0, 0)
        return group_blocks, from_neighbours(strided_blocks)

    group_blocks, shifted = exchange(dev_copies, grp_copies)
    near = near_part(0, group_blocks)
    second, dev_copies, grp_copies = far_part(1, shifted, near, first, basis)
    group_blocks, shifted = exchange(dev_copies, grp_copies)
    near = near_part(0, group_blocks)
    filtered, local_gram = far_part(2, shifted, near, second, first)

    def summed(parts, copies):
        return pl.pallas_call(
            sum_kernel,
            out_shape=jax.ShapeDtypeStruct((copies, 1, chunk_width), F32),
            in_specs=[vmem],
            out_specs=vmem,
            compiler_params=shared,
            name="sum_chunks",
        )(parts)

    parts = summed(lax.all_to_all(local_gram, "dev", 0, 0), group_count)
    parts = summed(lax.all_to_all(parts, "grp", 0, 0), group_size)
    parts = lax.all_to_all(parts, "dev", 0, 0)
    gram = pl.pallas_call(
        functools.partial(last_kernel, tile * group_size * group_count),
        out_shape=jax.ShapeDtypeStruct((width, width), F32),
        in_specs=[vmem],
        out_specs=vmem,
        compiler_params=shared,
        name="last_gram",
    )(parts)
    return filtered, gram


def solution(mesh):
    in_specs = (
        P(None, ("grp", "dev")),
        P(("grp", "dev"), None, None, None),
        P(("grp", "dev"), None),
        P(("grp", "dev"), None, None, None, None),
        P(("grp", "dev"), None, None),
        P(("grp", "dev"), None),
    )
    out_specs = (P(None, ("grp", "dev")), P())
    return jax.shard_map(
        on_device, mesh=mesh, in_specs=in_specs, out_specs=out_specs, check_vma=False
    )
```

```python
import functools

import jax
import jax.numpy as jnp
from jax import lax
from jax.experimental import pallas as pl
from jax.experimental.pallas import tpu as pltpu
from jax.sharding import PartitionSpec as P

STRIDE = 4
SHIFTS = {2: (1, -1), 4: (1, 2, -1)}[STRIDE]
UNROLL = 8
HEADER = 16
CUTS = 8
SHARED_VMEM = 16 * 1024 * 1024
WHOLE_VMEM = 60 * 1024 * 1024
BF16, F32, I32 = jnp.bfloat16, jnp.float32, jnp.int32


def add_tiles(total, blocks, tiles):
    return total + lax.dot_general(
        jnp.concatenate(blocks, axis=1),
        jnp.concatenate(tiles, axis=1),
        (((1,), (1,)), ((), ())),
        preferred_element_type=F32,
    )


def masked(block, live):
    return jnp.where(live, block, jnp.zeros_like(block))


def start_all(pairs, sem, first=0):
    copies = [
        pltpu.make_async_copy(source, target, sem.at[first + i])
        for i, (source, target) in enumerate(pairs)
    ]
    for copy in copies:
        copy.start()
    return copies


def cut(source, target, parts):
    step = max(1, target.shape[0] // parts)
    parts = target.shape[0] // step
    return [
        (source.at[pl.ds(i * step, step)], target.at[pl.ds(i * step, step)]) for i in range(parts)
    ]


def first_kernel(col, count, basis, help_, packed, rounded, block, copies, sem):
    group, tile_rows, tile = help_.shape
    rows, slots = basis.shape[0], col.shape[0]
    begun = start_all(
        [(basis, block)]
        + [(a, b) for a, b in cut(help_, copies.at[:, pl.ds(0, tile_rows)], CUTS)],
        sem,
    )
    lane = lax.broadcasted_iota(I32, (HEADER, tile), 1)

    def fill(p, carry):
        codes = jnp.full((HEADER, tile), -1, I32)
        for s in range(slots):
            codes = jnp.where(lane == s, jnp.where(s < count[0, p], col[s, p], -1), codes)
        copies[p, pl.ds(tile_rows + rows, HEADER)] = codes.astype(F32).astype(BF16)
        return carry

    lax.fori_loop(0, group, fill, 0)
    begun[0].wait()
    value = block[...].astype(BF16)
    rounded[...] = value
    copies[:, pl.ds(tile_rows, rows)] = jnp.broadcast_to(value[None], (group, rows, tile))
    ended = []
    for i, pair in enumerate(cut(copies, packed, CUTS)):
        begun[1 + i].wait()
        ended += start_all([pair], sem, 1 + CUTS + i)
    for copy in ended:
        copy.wait()


def near_kernel(at, code, lent, blocks, own, packed, out):
    group = packed.shape[0]
    rows, tile = out.shape
    slots = lent.shape[1]
    own_n = own.shape[0]
    total = jnp.zeros(out.shape, F32)

    def pick(c, live):
        return masked(blocks[jnp.where(live, c, 0), pl.ds(at, rows)], live)

    for t in range(0, own_n, UNROLL):
        codes = [code[0, i] for i in range(t, t + UNROLL)]
        total = add_tiles(
            total,
            [pick(c, c < group) for c in codes],
            [own[i] for i in range(t, t + UNROLL)],
        )
    for t in range(0, group * slots, UNROLL):
        places = [(i // slots, i % slots) for i in range(t, t + UNROLL)]
        codes = [lent[u, s] for u, s in places]
        total = add_tiles(
            total,
            [pick(c, c >= 0) for c in codes],
            [packed[u, pl.ds(s * tile, tile)] for u, s in places],
        )
    out[...] = total


def far_kernel(order, group, pieces, mine, code, *refs):
    parts, own, refs = refs[:pieces], refs[pieces], refs[pieces + 1 :]
    if order == 0:
        near, now, nxt, dev_out, grp_out = refs
    elif order == 1:
        near, now, before, nxt, dev_out, grp_out = refs
    else:
        near, now, before, nxt, gram = refs
    total_runs = parts[0].shape[0]

    def pick(c):
        live = c >= group
        far = jnp.where(live, c - group, 0)
        turn = lax.rem(far - mine[0] + STRIDE * total_runs, STRIDE)
        run = lax.div(far, STRIDE)
        found = masked(parts[0][run], live & (turn == 0))
        for i in range(1, STRIDE):
            found = jnp.where(live & (turn == i), parts[i][run], found)
        return found

    product = near[...]
    for t in range(0, own.shape[0], UNROLL):
        codes = [code[0, i] for i in range(t, t + UNROLL)]
        product = add_tiles(
            product, [pick(c) for c in codes], [own[i] for i in range(t, t + UNROLL)]
        )
    if order == 0:
        value = (product - 0.5 * now[...]) / 1.5
    else:
        value = 2.0 * (product - 0.5 * now[...]) / 1.5 - before[...]
    nxt[...] = value
    if order < 2:
        rounded = value.astype(BF16)
        dev_out[...] = rounded
        grp_out[...] = jnp.broadcast_to(rounded[None], grp_out.shape)
    else:
        whole = lax.dot_general(
            value,
            value,
            (((1,), (1,)), ((), ())),
            precision=lax.Precision.HIGHEST,
            preferred_element_type=F32,
        )
        n = gram.shape[0]
        rows = [whole[i : i + n] for i in range(0, whole.shape[0], n)]
        gram[...] = jnp.concatenate(rows, axis=1).reshape(gram.shape)


def sum_kernel(parts, out):
    out[...] = jnp.broadcast_to(jnp.sum(parts[...], axis=0, keepdims=True), out.shape)


def last_kernel(nodes, parts, out):
    whole = parts[...].reshape(parts.shape[0], parts.shape[2]) / nodes
    n, width = whole.shape[0], out.shape[1]
    for i in range(out.shape[0] // n):
        out[pl.ds(i * n, n)] = whole[:, i * width : (i + 1) * width]


def on_device(basis, own_tiles, own_col, help_tiles, help_col, help_count):
    width, tile = basis.shape
    group_size = lax.axis_size("dev")
    group_count = lax.axis_size("grp")
    slots = help_tiles.shape[2]
    own_n = own_tiles.shape[1]
    runs = group_count // STRIDE
    mine = lax.axis_index("grp").astype(I32)[None]
    vmem = pl.BlockSpec(memory_space=pltpu.VMEM)
    smem = pl.BlockSpec(memory_space=pltpu.SMEM)
    hbm = pl.BlockSpec(memory_space=pltpu.HBM)
    anywhere = pl.BlockSpec(memory_space=pl.ANY)
    whole = pltpu.CompilerParams(vmem_limit_bytes=WHOLE_VMEM)
    shared = pltpu.CompilerParams(vmem_limit_bytes=SHARED_VMEM)
    strided = [[b + STRIDE * a for a in range(runs)] for b in range(STRIDE)]
    block = jax.ShapeDtypeStruct((width, tile), F32)
    tile_rows = slots * tile

    packed, rounded = pl.pallas_call(
        first_kernel,
        out_shape=(
            jax.ShapeDtypeStruct((group_size, tile_rows + width + HEADER, tile), BF16),
            jax.ShapeDtypeStruct((width, tile), BF16),
        ),
        in_specs=[smem, smem, anywhere, anywhere],
        out_specs=(hbm, vmem),
        scratch_shapes=[
            pltpu.VMEM((width, tile), F32),
            pltpu.VMEM((group_size, tile_rows + width + HEADER, tile), BF16),
            pltpu.SemaphoreType.DMA((1 + 2 * CUTS,)),
        ],
        compiler_params=whole,
        name="first_copies",
    )(help_col[0].T, help_count, basis, help_tiles[0].reshape(group_size, tile_rows, tile))

    def from_neighbours(strided_blocks):
        shifted = [strided_blocks]
        for n, shift in enumerate(SHIFTS):
            piece = strided_blocks
            if STRIDE == 2:
                piece = strided_blocks[n * (runs // 2) : (n + 1) * (runs // 2)]
            pairs = [(i, (i - shift) % group_count) for i in range(group_count)]
            shifted.append(lax.ppermute(piece, "grp", pairs))
        return shifted

    def near_part(at, blocks):
        return pl.pallas_call(
            functools.partial(near_kernel, at),
            out_shape=block,
            in_specs=[smem, smem, vmem, vmem, vmem],
            out_specs=vmem,
            compiler_params=shared,
            cost_estimate=pl.CostEstimate(
                flops=2 * width * tile * tile * (own_n + group_size * slots),
                bytes_accessed=2 * tile * tile * (own_n + group_size * slots),
                transcendentals=0,
            ),
            name="near_tiles",
        )(own_col, lent, blocks, own_tiles[0], packed)

    chunk_width = width * width // group_size

    def far_part(order, shifted, *states):
        out_shape = [block]
        if order < 2:
            out_shape.append(jax.ShapeDtypeStruct((width, tile), BF16))
            out_shape.append(jax.ShapeDtypeStruct((runs, width, tile), BF16))
        else:
            out_shape.append(jax.ShapeDtypeStruct((group_size, 1, chunk_width), F32))
        return pl.pallas_call(
            functools.partial(far_kernel, order, group_size, len(shifted)),
            out_shape=tuple(out_shape),
            in_specs=[smem, smem] + [vmem] * (len(shifted) + 1 + len(states)),
            out_specs=(vmem,) * len(out_shape),
            compiler_params=shared,
            name="far_tiles",
        )(mine, own_col, *shifted, own_tiles[0], *states)

    packed = lax.all_to_all(packed, "dev", 0, 0)
    strided_blocks = lax.all_gather(rounded, "grp", axis=0, axis_index_groups=strided)
    shifted = from_neighbours(strided_blocks)
    lent = packed[:, tile_rows + width, :slots].astype(I32)
    near = near_part(tile_rows, packed)
    first, rounded, grp_copies = far_part(0, shifted, near, basis)

    def exchange(rounded, grp_copies):
        strided_blocks = lax.all_to_all(grp_copies, "grp", 0, 0, axis_index_groups=strided)
        group_blocks = lax.all_gather(rounded, "dev", axis=0)
        strided_blocks, group_blocks = lax.optimization_barrier((strided_blocks, group_blocks))
        return group_blocks, from_neighbours(strided_blocks)

    group_blocks, shifted = exchange(rounded, grp_copies)
    near = near_part(0, group_blocks)
    second, rounded, grp_copies = far_part(1, shifted, near, first, basis)
    group_blocks, shifted = exchange(rounded, grp_copies)
    near = near_part(0, group_blocks)
    filtered, local_gram = far_part(2, shifted, near, second, first)

    def summed(parts, copies):
        return pl.pallas_call(
            sum_kernel,
            out_shape=jax.ShapeDtypeStruct((copies, 1, chunk_width), F32),
            in_specs=[vmem],
            out_specs=vmem,
            compiler_params=shared,
            name="sum_chunks",
        )(parts)

    parts = summed(lax.all_to_all(local_gram, "dev", 0, 0), group_count)
    parts = summed(lax.all_to_all(parts, "grp", 0, 0), group_size)
    parts = lax.all_to_all(parts, "dev", 0, 0)
    gram = pl.pallas_call(
        functools.partial(last_kernel, tile * group_size * group_count),
        out_shape=jax.ShapeDtypeStruct((width, width), F32),
        in_specs=[vmem],
        out_specs=vmem,
        compiler_params=shared,
        name="last_gram",
    )(parts)
    return filtered, gram


def solution(mesh):
    in_specs = (
        P(None, ("grp", "dev")),
        P(("grp", "dev"), None, None, None),
        P(("grp", "dev"), None),
        P(("grp", "dev"), None, None, None, None),
        P(("grp", "dev"), None, None),
        P(("grp", "dev"), None),
    )
    out_specs = (P(None, ("grp", "dev")), P())
    return jax.shard_map(
        on_device, mesh=mesh, in_specs=in_specs, out_specs=out_specs, check_vma=False
    )
```

```python
import functools

import jax
import jax.numpy as jnp
from jax import lax
from jax.experimental import pallas as pl
from jax.experimental.pallas import tpu as pltpu
from jax.sharding import PartitionSpec as P

STRIDE = 4
SHIFTS = {2: (1, -1), 4: (1, 2, -1)}[STRIDE]
UNROLL = 8
HEADER = 16
CUTS = 8
SHARED_VMEM = 16 * 1024 * 1024
WHOLE_VMEM = 60 * 1024 * 1024
BF16, F32, I32 = jnp.bfloat16, jnp.float32, jnp.int32


def add_tiles(total, blocks, tiles):
    return total + lax.dot_general(
        jnp.concatenate(blocks, axis=1),
        jnp.concatenate(tiles, axis=1),
        (((1,), (1,)), ((), ())),
        preferred_element_type=F32,
    )


def masked(block, live):
    return jnp.where(live, block, jnp.zeros_like(block))


def start_all(pairs, sem, first=0):
    copies = [
        pltpu.make_async_copy(source, target, sem.at[first + i])
        for i, (source, target) in enumerate(pairs)
    ]
    for copy in copies:
        copy.start()
    return copies


def cut(source, target, parts):
    step = max(1, target.shape[0] // parts)
    parts = target.shape[0] // step
    return [
        (source.at[pl.ds(i * step, step)], target.at[pl.ds(i * step, step)]) for i in range(parts)
    ]


def first_kernel(col_at, count_at, basis, help_, packed, rounded, col, count, block, copies, sem):
    group, tile_rows, tile = help_.shape
    rows, slots = basis.shape[0], col_at.shape[0]
    begun = start_all(
        [(basis, block)]
        + [(a, b) for a, b in cut(help_, copies.at[:, pl.ds(0, tile_rows)], CUTS)],
        sem,
    )
    scalars = start_all([(col_at, col), (count_at, count)], sem, 1 + 2 * CUTS)
    lane = lax.broadcasted_iota(I32, (HEADER, tile), 1)

    def fill(p, carry):
        codes = jnp.full((HEADER, tile), -1, I32)
        for s in range(slots):
            codes = jnp.where(lane == s, jnp.where(s < count[0, p], col[s, p], -1), codes)
        copies[p, pl.ds(tile_rows + rows, HEADER)] = codes.astype(F32).astype(BF16)
        return carry

    begun[0].wait()
    value = block[...].astype(BF16)
    rounded[...] = value
    copies[:, pl.ds(tile_rows, rows)] = jnp.broadcast_to(value[None], (group, rows, tile))
    for copy in scalars:
        copy.wait()
    lax.fori_loop(0, group, fill, 0)
    ended = []
    for i, pair in enumerate(cut(copies, packed, CUTS)):
        begun[1 + i].wait()
        ended += start_all([pair], sem, 1 + CUTS + i)
    for copy in ended:
        copy.wait()


def help_kernel(at, lent, blocks, packed, out):
    rows, tile = out.shape
    slots = lent.shape[1]
    total = jnp.zeros(out.shape, F32)
    for t in range(0, packed.shape[0] * slots, UNROLL):
        places = [(i // slots, i % slots) for i in range(t, t + UNROLL)]
        codes = [lent[u, s] for u, s in places]
        total = add_tiles(
            total,
            [masked(blocks[jnp.where(c >= 0, c, 0), pl.ds(at, rows)], c >= 0) for c in codes],
            [packed[u, pl.ds(s * tile, tile)] for u, s in places],
        )
    out[...] = total


def own_kernel(order, at, pieces, mine, code, blocks, *refs):
    parts, own, refs = refs[:pieces], refs[pieces], refs[pieces + 1 :]
    if order == 0:
        near, now, nxt, dev_out, grp_out = refs
    elif order == 1:
        near, now, before, nxt, dev_out, grp_out = refs
    else:
        near, now, before, nxt, gram = refs
    group, rows, total_runs = blocks.shape[0], near.shape[0], parts[0].shape[0]

    def pick(c):
        live = c >= group
        far = jnp.where(live, c - group, 0)
        turn = lax.rem(far - mine[0] + STRIDE * total_runs, STRIDE)
        run = lax.div(far, STRIDE)
        found = blocks[jnp.where(live, 0, c), pl.ds(at, rows)]
        for i in range(STRIDE):
            found = jnp.where(live & (turn == i), parts[i][run], found)
        return found

    product = near[...]
    for t in range(0, own.shape[0], UNROLL):
        codes = [code[0, i] for i in range(t, t + UNROLL)]
        product = add_tiles(
            product, [pick(c) for c in codes], [own[i] for i in range(t, t + UNROLL)]
        )
    if order == 0:
        value = (product - 0.5 * now[...]) / 1.5
    else:
        value = 2.0 * (product - 0.5 * now[...]) / 1.5 - before[...]
    nxt[...] = value
    if order < 2:
        rounded = value.astype(BF16)[None]
        dev_out[...] = jnp.broadcast_to(rounded, dev_out.shape)
        grp_out[...] = jnp.broadcast_to(rounded, grp_out.shape)
    else:
        whole = lax.dot_general(
            value,
            value,
            (((1,), (1,)), ((), ())),
            precision=lax.Precision.HIGHEST,
            preferred_element_type=F32,
        )
        n = gram.shape[0]
        rows = [whole[i : i + n] for i in range(0, whole.shape[0], n)]
        gram[...] = jnp.concatenate(rows, axis=1).reshape(gram.shape)


def sum_kernel(parts, out):
    out[...] = jnp.broadcast_to(jnp.sum(parts[...], axis=0, keepdims=True), out.shape)


def last_kernel(nodes, parts, out):
    whole = parts[...].reshape(parts.shape[0], parts.shape[2]) / nodes
    n, width = whole.shape[0], out.shape[1]
    for i in range(out.shape[0] // n):
        out[pl.ds(i * n, n)] = whole[:, i * width : (i + 1) * width]


def on_device(basis, own_tiles, own_col, help_tiles, help_col, help_count):
    width, tile = basis.shape
    group_size = lax.axis_size("dev")
    group_count = lax.axis_size("grp")
    slots = help_tiles.shape[2]
    own_n = own_tiles.shape[1]
    runs = group_count // STRIDE
    mine = lax.axis_index("grp").astype(I32)[None]
    vmem = pl.BlockSpec(memory_space=pltpu.VMEM)
    smem = pl.BlockSpec(memory_space=pltpu.SMEM)
    hbm = pl.BlockSpec(memory_space=pltpu.HBM)
    anywhere = pl.BlockSpec(memory_space=pl.ANY)
    whole = pltpu.CompilerParams(vmem_limit_bytes=WHOLE_VMEM)
    shared = pltpu.CompilerParams(vmem_limit_bytes=SHARED_VMEM)
    strided = [[b + STRIDE * a for a in range(runs)] for b in range(STRIDE)]
    block = jax.ShapeDtypeStruct((width, tile), F32)
    tile_rows = slots * tile

    packed, rounded = pl.pallas_call(
        first_kernel,
        out_shape=(
            jax.ShapeDtypeStruct((group_size, tile_rows + width + HEADER, tile), BF16),
            jax.ShapeDtypeStruct((width, tile), BF16),
        ),
        in_specs=[anywhere] * 4,
        out_specs=(hbm, vmem),
        scratch_shapes=[
            pltpu.SMEM((slots, group_size), I32),
            pltpu.SMEM((1, group_size), I32),
            pltpu.VMEM((width, tile), F32),
            pltpu.VMEM((group_size, tile_rows + width + HEADER, tile), BF16),
            pltpu.SemaphoreType.DMA((3 + 2 * CUTS,)),
        ],
        compiler_params=whole,
        name="first_copies",
    )(help_col[0].T, help_count, basis, help_tiles[0].reshape(group_size, tile_rows, tile))

    def from_neighbours(strided_blocks):
        shifted = [strided_blocks]
        for n, shift in enumerate(SHIFTS):
            piece = strided_blocks
            if STRIDE == 2:
                piece = strided_blocks[n * (runs // 2) : (n + 1) * (runs // 2)]
            turns = [shift if i % 2 or abs(shift) == 1 else -shift for i in range(group_count)]
            pairs = [(i, (i - turn) % group_count) for i, turn in enumerate(turns)]
            shifted.append(lax.ppermute(piece, "grp", pairs))
        return shifted

    def help_part(at, blocks):
        return pl.pallas_call(
            functools.partial(help_kernel, at),
            out_shape=block,
            in_specs=[smem, vmem, vmem],
            out_specs=vmem,
            compiler_params=shared,
            cost_estimate=pl.CostEstimate(
                flops=2 * width * tile * tile * group_size * slots,
                bytes_accessed=2 * tile * tile * group_size * slots,
                transcendentals=0,
            ),
            name="help_tiles",
        )(lent, blocks, packed)

    chunk_width = width * width // group_size

    def own_part(order, at, blocks, shifted, *states):
        out_shape = [block]
        if order < 2:
            out_shape.append(jax.ShapeDtypeStruct((group_size, width, tile), BF16))
            out_shape.append(jax.ShapeDtypeStruct((runs, width, tile), BF16))
        else:
            out_shape.append(jax.ShapeDtypeStruct((group_size, 1, chunk_width), F32))
        return pl.pallas_call(
            functools.partial(own_kernel, order, at, len(shifted)),
            out_shape=tuple(out_shape),
            in_specs=[smem, smem] + [vmem] * (len(shifted) + 2 + len(states)),
            out_specs=(vmem,) * len(out_shape),
            compiler_params=shared,
            name="own_tiles",
        )(mine, own_col, blocks, *shifted, own_tiles[0], *states)

    packed = lax.all_to_all(packed, "dev", 0, 0)
    strided_blocks = lax.all_gather(rounded, "grp", axis=0, axis_index_groups=strided)
    shifted = from_neighbours(strided_blocks)
    lent = packed[:, tile_rows + width, :slots].astype(I32)
    near = help_part(tile_rows, packed)
    first, dev_copies, grp_copies = own_part(0, tile_rows, packed, shifted, near, basis)

    def exchange(dev_copies, grp_copies):
        strided_blocks = lax.all_to_all(grp_copies, "grp", 0, 0, axis_index_groups=strided)
        group_blocks = lax.all_to_all(dev_copies, "dev", 0, 0)
        return group_blocks, from_neighbours(strided_blocks)

    group_blocks, shifted = exchange(dev_copies, grp_copies)
    near = help_part(0, group_blocks)
    second, dev_copies, grp_copies = own_part(1, 0, group_blocks, shifted, near, first, basis)
    group_blocks, shifted = exchange(dev_copies, grp_copies)
    near = help_part(0, group_blocks)
    filtered, local_gram = own_part(2, 0, group_blocks, shifted, near, second, first)

    def summed(parts, copies):
        return pl.pallas_call(
            sum_kernel,
            out_shape=jax.ShapeDtypeStruct((copies, 1, chunk_width), F32),
            in_specs=[vmem],
            out_specs=vmem,
            compiler_params=shared,
            name="sum_chunks",
        )(parts)

    parts = summed(lax.all_to_all(local_gram, "dev", 0, 0), group_count)
    parts = summed(lax.all_to_all(parts, "grp", 0, 0), group_size)
    parts = lax.all_to_all(parts, "dev", 0, 0)
    gram = pl.pallas_call(
        functools.partial(last_kernel, tile * group_size * group_count),
        out_shape=jax.ShapeDtypeStruct((width, width), F32),
        in_specs=[vmem],
        out_specs=vmem,
        compiler_params=shared,
        name="last_gram",
    )(parts)
    return filtered, gram


def solution(mesh):
    in_specs = (
        P(None, ("grp", "dev")),
        P(("grp", "dev"), None, None, None),
        P(("grp", "dev"), None),
        P(("grp", "dev"), None, None, None, None),
        P(("grp", "dev"), None, None),
        P(("grp", "dev"), None),
    )
    out_specs = (P(None, ("grp", "dev")), P())
    return jax.shard_map(
        on_device, mesh=mesh, in_specs=in_specs, out_specs=out_specs, check_vma=False
    )
```

```python
import functools

import jax
import jax.numpy as jnp
from jax import lax
from jax.experimental import pallas as pl
from jax.experimental.pallas import tpu as pltpu
from jax.sharding import PartitionSpec as P

STRIDE = 4
SHIFTS = (2, 1, -1)
TURNS = (0, *(shift % STRIDE for shift in SHIFTS))
UNROLL = 8
HEADER = 16
CUTS = 8
SHARED_VMEM = 16 * 1024 * 1024
WHOLE_VMEM = 60 * 1024 * 1024
BF16, F32, I32 = jnp.bfloat16, jnp.float32, jnp.int32


def add_tiles(total, blocks, tiles):
    return total + lax.dot_general(
        jnp.concatenate(blocks, axis=1),
        jnp.concatenate(tiles, axis=1),
        (((1,), (1,)), ((), ())),
        preferred_element_type=F32,
    )


def masked(block, live):
    return jnp.where(live, block, jnp.zeros_like(block))


def start_all(pairs, sem, first=0):
    copies = [
        pltpu.make_async_copy(source, target, sem.at[first + i])
        for i, (source, target) in enumerate(pairs)
    ]
    for copy in copies:
        copy.start()
    return copies


def cut(source, target, parts):
    step = max(1, target.shape[0] // parts)
    parts = target.shape[0] // step
    return [
        (source.at[pl.ds(i * step, step)], target.at[pl.ds(i * step, step)]) for i in range(parts)
    ]


def first_kernel(col_at, count_at, basis, help_, packed, rounded, col, count, block, copies, sem):
    group, tile_rows, tile = help_.shape
    rows, slots = basis.shape[0], col_at.shape[0]
    begun = start_all(
        [(basis, block)]
        + [(a, b) for a, b in cut(help_, copies.at[:, pl.ds(0, tile_rows)], CUTS)],
        sem,
    )
    scalars = start_all([(col_at, col), (count_at, count)], sem, 1 + 2 * CUTS)
    lane = lax.broadcasted_iota(I32, (HEADER, tile), 1)

    def fill(p, carry):
        codes = jnp.full((HEADER, tile), -1, I32)
        for s in range(slots):
            codes = jnp.where(lane == s, jnp.where(s < count[0, p], col[s, p], -1), codes)
        copies[p, pl.ds(tile_rows + rows, HEADER)] = codes.astype(F32).astype(BF16)
        return carry

    begun[0].wait()
    value = block[...].astype(BF16)
    rounded[...] = value
    copies[:, pl.ds(tile_rows, rows)] = jnp.broadcast_to(value[None], (group, rows, tile))
    for copy in scalars:
        copy.wait()
    lax.fori_loop(0, group, fill, 0)
    ended = []
    for i, pair in enumerate(cut(copies, packed, CUTS)):
        begun[1 + i].wait()
        ended += start_all([pair], sem, 1 + CUTS + i)
    for copy in ended:
        copy.wait()


def help_kernel(at, lent, blocks, packed, out):
    rows, tile = out.shape
    slots = lent.shape[1]
    total = jnp.zeros(out.shape, F32)
    for t in range(0, packed.shape[0] * slots, UNROLL):
        places = [(i // slots, i % slots) for i in range(t, t + UNROLL)]
        codes = [lent[u, s] for u, s in places]
        total = add_tiles(
            total,
            [masked(blocks[jnp.where(c >= 0, c, 0), pl.ds(at, rows)], c >= 0) for c in codes],
            [packed[u, pl.ds(s * tile, tile)] for u, s in places],
        )
    out[...] = total


def own_kernel(order, at, pieces, mine, code, blocks, *refs):
    parts, own, refs = refs[:pieces], refs[pieces], refs[pieces + 1 :]
    if order == 0:
        near, now, nxt, dev_out, grp_out = refs
    elif order == 1:
        near, now, before, nxt, dev_out, grp_out = refs
    else:
        near, now, before, nxt, gram = refs
    group, rows, total_runs = blocks.shape[0], near.shape[0], parts[0].shape[0]

    def pick(c):
        live = c >= group
        far = jnp.where(live, c - group, 0)
        turn = lax.rem(far - mine[0] + STRIDE * total_runs, STRIDE)
        run = lax.div(far, STRIDE)
        found = blocks[jnp.where(live, 0, c), pl.ds(at, rows)]
        for i, part in zip(TURNS, parts):
            found = jnp.where(live & (turn == i), part[run], found)
        return found

    product = near[...]
    for t in range(0, own.shape[0], UNROLL):
        codes = [code[0, i] for i in range(t, t + UNROLL)]
        product = add_tiles(
            product, [pick(c) for c in codes], [own[i] for i in range(t, t + UNROLL)]
        )
    if order == 0:
        value = (product - 0.5 * now[...]) / 1.5
    else:
        value = 2.0 * (product - 0.5 * now[...]) / 1.5 - before[...]
    nxt[...] = value
    if order < 2:
        rounded = value.astype(BF16)[None]
        dev_out[...] = jnp.broadcast_to(rounded, dev_out.shape)
        grp_out[...] = jnp.broadcast_to(rounded, grp_out.shape)
    else:
        whole = lax.dot_general(
            value,
            value,
            (((1,), (1,)), ((), ())),
            precision=lax.Precision.HIGHEST,
            preferred_element_type=F32,
        )
        n = gram.shape[0]
        rows = [whole[i : i + n] for i in range(0, whole.shape[0], n)]
        gram[...] = jnp.concatenate(rows, axis=1).reshape(gram.shape)


def sum_kernel(parts, out):
    out[...] = jnp.broadcast_to(jnp.sum(parts[...], axis=0, keepdims=True), out.shape)


def last_kernel(nodes, parts, out):
    whole = parts[...].reshape(parts.shape[0], parts.shape[2]) / nodes
    n, width = whole.shape[0], out.shape[1]
    for i in range(out.shape[0] // n):
        out[pl.ds(i * n, n)] = whole[:, i * width : (i + 1) * width]


def on_device(basis, own_tiles, own_col, help_tiles, help_col, help_count):
    width, tile = basis.shape
    group_size = lax.axis_size("dev")
    group_count = lax.axis_size("grp")
    slots = help_tiles.shape[2]
    own_n = own_tiles.shape[1]
    runs = group_count // STRIDE
    mine = lax.axis_index("grp").astype(I32)[None]
    vmem = pl.BlockSpec(memory_space=pltpu.VMEM)
    smem = pl.BlockSpec(memory_space=pltpu.SMEM)
    hbm = pl.BlockSpec(memory_space=pltpu.HBM)
    anywhere = pl.BlockSpec(memory_space=pl.ANY)
    whole = pltpu.CompilerParams(vmem_limit_bytes=WHOLE_VMEM)
    shared = pltpu.CompilerParams(vmem_limit_bytes=SHARED_VMEM)
    strided = [[b + STRIDE * a for a in range(runs)] for b in range(STRIDE)]
    block = jax.ShapeDtypeStruct((width, tile), F32)
    tile_rows = slots * tile

    packed, rounded = pl.pallas_call(
        first_kernel,
        out_shape=(
            jax.ShapeDtypeStruct((group_size, tile_rows + width + HEADER, tile), BF16),
            jax.ShapeDtypeStruct((width, tile), BF16),
        ),
        in_specs=[anywhere] * 4,
        out_specs=(hbm, vmem),
        scratch_shapes=[
            pltpu.SMEM((slots, group_size), I32),
            pltpu.SMEM((1, group_size), I32),
            pltpu.VMEM((width, tile), F32),
            pltpu.VMEM((group_size, tile_rows + width + HEADER, tile), BF16),
            pltpu.SemaphoreType.DMA((3 + 2 * CUTS,)),
        ],
        compiler_params=whole,
        name="first_copies",
    )(help_col[0].T, help_count, basis, help_tiles[0].reshape(group_size, tile_rows, tile))

    def from_neighbours(strided_blocks):
        shifted = {0: strided_blocks}
        for shift in SHIFTS:
            turns = [shift if i % 2 or abs(shift) == 1 else -shift for i in range(group_count)]
            pairs = [(i, (i - turn) % group_count) for i, turn in enumerate(turns)]
            shifted[shift % STRIDE] = lax.ppermute(strided_blocks, "grp", pairs)
        return [shifted[turn] for turn in TURNS]

    def help_part(at, blocks):
        return pl.pallas_call(
            functools.partial(help_kernel, at),
            out_shape=block,
            in_specs=[smem, vmem, vmem],
            out_specs=vmem,
            compiler_params=shared,
            cost_estimate=pl.CostEstimate(
                flops=2 * width * tile * tile * group_size * slots,
                bytes_accessed=2 * tile * tile * group_size * slots,
                transcendentals=0,
            ),
            name="help_tiles",
        )(lent, blocks, packed)

    chunk_width = width * width // group_size

    def own_part(order, at, blocks, shifted, *states):
        out_shape = [block]
        if order < 2:
            out_shape.append(jax.ShapeDtypeStruct((group_size, width, tile), BF16))
            out_shape.append(jax.ShapeDtypeStruct((runs, width, tile), BF16))
        else:
            out_shape.append(jax.ShapeDtypeStruct((group_size, 1, chunk_width), F32))
        return pl.pallas_call(
            functools.partial(own_kernel, order, at, len(shifted)),
            out_shape=tuple(out_shape),
            in_specs=[smem, smem] + [vmem] * (len(shifted) + 2 + len(states)),
            out_specs=(vmem,) * len(out_shape),
            compiler_params=shared,
            name="own_tiles",
        )(mine, own_col, blocks, *shifted, own_tiles[0], *states)

    packed = lax.all_to_all(packed, "dev", 0, 0)
    strided_blocks = lax.all_gather(rounded, "grp", axis=0, axis_index_groups=strided)
    shifted = from_neighbours(strided_blocks)
    lent = packed[:, tile_rows + width, :slots].astype(I32)
    near = help_part(tile_rows, packed)
    first, dev_copies, grp_copies = own_part(0, tile_rows, packed, shifted, near, basis)

    def exchange(dev_copies, grp_copies):
        strided_blocks = lax.all_to_all(grp_copies, "grp", 0, 0, axis_index_groups=strided)
        group_blocks = lax.all_to_all(dev_copies, "dev", 0, 0)
        return group_blocks, from_neighbours(strided_blocks)

    group_blocks, shifted = exchange(dev_copies, grp_copies)
    near = help_part(0, group_blocks)
    second, dev_copies, grp_copies = own_part(1, 0, group_blocks, shifted, near, first, basis)
    group_blocks, shifted = exchange(dev_copies, grp_copies)
    near = help_part(0, group_blocks)
    filtered, local_gram = own_part(2, 0, group_blocks, shifted, near, second, first)

    def summed(parts, copies):
        return pl.pallas_call(
            sum_kernel,
            out_shape=jax.ShapeDtypeStruct((copies, 1, chunk_width), F32),
            in_specs=[vmem],
            out_specs=vmem,
            compiler_params=shared,
            name="sum_chunks",
        )(parts)

    parts = summed(lax.all_to_all(local_gram, "dev", 0, 0), group_count)
    parts = summed(lax.all_to_all(parts, "grp", 0, 0), group_size)
    parts = lax.all_to_all(parts, "dev", 0, 0)
    gram = pl.pallas_call(
        functools.partial(last_kernel, tile * group_size * group_count),
        out_shape=jax.ShapeDtypeStruct((width, width), F32),
        in_specs=[vmem],
        out_specs=vmem,
        compiler_params=shared,
        name="last_gram",
    )(parts)
    return filtered, gram


def solution(mesh):
    in_specs = (
        P(None, ("grp", "dev")),
        P(("grp", "dev"), None, None, None),
        P(("grp", "dev"), None),
        P(("grp", "dev"), None, None, None, None),
        P(("grp", "dev"), None, None),
        P(("grp", "dev"), None),
    )
    out_specs = (P(None, ("grp", "dev")), P())
    return jax.shard_map(
        on_device, mesh=mesh, in_specs=in_specs, out_specs=out_specs, check_vma=False
    )
```
